32 devices in a mesh: row: 4 (over z), col: 8 (over y, x, core).
Axes of the slice: x: 2, y: 2, z: 4, core: 2. Of those that a mesh axis runs over, the one named last changes fastest.
Arguments:
- queries: bfloat16 [1024, 4096], P(('row', 'col')), may hold values from -8 to 8
- passages: bfloat16 [16384, 4096], P(('row', 'col')), may hold values from -8 to 8
- adapter: bfloat16 [4096, 768], replicated, may hold values from -0.09375 to 0.09375
- positives: int32 [1024], replicated, may hold values from 0 to 16383
Outputs:
- adapter_grad: float32 [4096, 768], P(('row', 'col'))
- query_grad: bfloat16 [1024, 4096], P(('row', 'col'))
- losses: float32 [1024], P(('row', 'col'))
The draws below stay inside these ranges and needn't reach their ends.
All inputs are finite; a program needn't handle non-finite values.
Results may differ from the reference program's by a relative error of at most 0.0088.
Values may be sent and summed in bfloat16 or wider, within the bound.
A program may use at most 128 MiB of HBM per device.

```python
import jax
import jax.numpy as jnp
from jax import lax

DIN = 4096
E = 768
PASS_DEV = 512
QUERIES = 1024
PASSAGES = 16384


def cluster_centres(key):
    inner = jax.random.fold_in(key, 5)
    return jax.random.normal(jax.random.fold_in(inner, 1), (256, DIN), jnp.float32)


def cluster_shift(key, salt, count):
    centres = cluster_centres(key)
    labels = jax.random.randint(jax.random.fold_in(jax.random.fold_in(key, 6), salt), (count,), 0, 256)
    return 0.5 * centres[labels]


def draw_queries(key, part):
    shift = cluster_shift(key, 1, QUERIES)
    noise = jax.random.normal(jax.random.fold_in(key, 22), (QUERIES, DIN), jnp.float32)
    values = jnp.clip(shift + 0.87 * noise, -8.0, 8.0)
    return values.astype(jnp.bfloat16)


def draw_passages(key, part):
    shift = cluster_shift(key, 2, PASSAGES)
    noise = jax.random.normal(jax.random.fold_in(key, 32), (PASSAGES, DIN), jnp.float32)
    values = jnp.clip(shift + 0.87 * noise, -8.0, 8.0)
    return values.astype(jnp.bfloat16)


def plant(values, own_key, least, largest):
    longest = values.shape.index(max(values.shape))
    spots = []
    for shift in (0, 1):
        where = [jax.random.randint(jax.random.fold_in(own_key, axis), (), 0, length) for axis, length in enumerate(values.shape)]
        where[longest] = (where[longest] + shift) % values.shape[longest]
        spots.append(tuple(where))
    return values.at[spots[0]].set(least).at[spots[1]].set(largest)


def bell_draw(stream_key, dims, scale, most, held_as=jnp.bfloat16):
    drawn = jax.random.normal(stream_key, dims, jnp.float32) * scale
    return jnp.minimum(jnp.maximum(drawn, -most), most).astype(held_as)


def setup_inputs(seed: int = 0) -> dict:
    streams_of = jax.random.split(jax.random.key(seed), 5)
    queries = draw_queries(jax.random.fold_in(streams_of[4], 71), 0)
    passages = draw_passages(jax.random.fold_in(streams_of[4], 71), 0)
    adapter = bell_draw(streams_of[2], (DIN, E), DIN ** -0.5, 0.09375)
    positives = plant(jax.random.randint(streams_of[3], (QUERIES,), 0, PASSAGES), jax.random.fold_in(streams_of[3], 1), 0, PASSAGES - 1).astype(jnp.int32)
    return {"queries": queries, "passages": passages, "adapter": adapter, "positives": positives}


def reference(queries, passages, adapter, positives):
    scale = adapter.shape[1] ** -0.5
    width = queries.shape[1]
    qa = jnp.dot(queries, adapter, preferred_element_type=jnp.float32).astype(jnp.bfloat16)
    slabs = passages.reshape(-1, PASS_DEV, width)
    count = slabs.shape[0]
    nquery = queries.shape[0]

    def score(pa, index):
        values = jnp.dot(qa, pa.T, preferred_element_type=jnp.float32) * scale
        columns = index * PASS_DEV + jnp.arange(PASS_DEV, dtype=jnp.int32)
        return values, positives[:, None] == columns[None, :]

    def first(carry, item):
        top, total, picked = carry
        slab, index = item
        pa = jnp.dot(slab, adapter, preferred_element_type=jnp.float32).astype(jnp.bfloat16)
        values, hit = score(pa, index)
        newtop = jnp.maximum(top, jnp.max(values, axis=1))
        total = total * jnp.exp(top - newtop) + jnp.sum(jnp.exp(values - newtop[:, None]), axis=1)
        picked = picked + jnp.sum(jnp.where(hit, values, 0.0), axis=1)
        return (newtop, total, picked), pa

    start = (jnp.full((nquery,), -jnp.inf, jnp.float32), jnp.zeros((nquery,), jnp.float32), jnp.zeros((nquery,), jnp.float32))
    indices = jnp.arange(count, dtype=jnp.int32)
    (top, total, picked), projected = lax.scan(first, start, (slabs, indices))
    lse = top + jnp.log(total)

    def second(carry, item):
        dqa, dweight = carry
        slab, pa, index = item
        values, hit = score(pa, index)
        probs = jnp.exp(values - lse[:, None])
        dscores = ((probs - hit.astype(jnp.float32)) * scale).astype(jnp.bfloat16)
        dqa = dqa + jnp.dot(dscores, pa, preferred_element_type=jnp.float32)
        dpa = jnp.dot(dscores.T, qa, preferred_element_type=jnp.float32).astype(jnp.bfloat16)
        dweight = dweight + jnp.dot(slab.T, dpa, preferred_element_type=jnp.float32)
        return (dqa, dweight), None

    init = (jnp.zeros((nquery, adapter.shape[1]), jnp.float32), jnp.zeros(adapter.shape, jnp.float32))
    (dqa, dweight), unused = lax.scan(second, init, (slabs, projected, indices))
    dqa_low = dqa.astype(jnp.bfloat16)
    dweight = dweight + jnp.dot(queries.T, dqa_low, preferred_element_type=jnp.float32)
    query_grad = jnp.dot(dqa_low, adapter.T, preferred_element_type=jnp.float32).astype(jnp.bfloat16)
    return dweight, query_grad, lse - picked
```

```python
import functools

import jax
import jax.numpy as jnp
from jax import lax
from jax.experimental import pallas as pl
from jax.experimental.pallas import tpu as pltpu
from jax.sharding import PartitionSpec as P

MESH = pl.DeviceIdType.MESH
LIMIT = 56 * 1024 * 1024


class Grid:
    def __init__(self, n_row, n_col):
        factors, left = [], n_col
        while left % 2 == 0:
            factors.append(2)
            left //= 2
        if left > 1:
            factors.insert(0, left)
        self.sizes = [n_row] + factors[::-1] if left == 1 else [n_row] + factors
        self.n_row, self.n_col = n_row, n_col
        self.core = len(self.sizes) - 1
        self.strides = [0] * len(self.sizes)
        stride = 1
        for dim in range(self.core, 0, -1):
            self.strides[dim] = stride
            stride *= self.sizes[dim]

    def place(self):
        row, col = lax.axis_index("row"), lax.axis_index("col")
        mine = [row]
        for dim in range(1, self.core + 1):
            mine.append(lax.rem(col // self.strides[dim], self.sizes[dim]))
        return row, col, mine

    def partner(self, row, col, mine, dim, value):
        if dim == 0:
            return (value, col)
        return (row, col + (value - mine[dim]) * self.strides[dim])

    def moved(self, mine, dim, offset):
        size = self.sizes[dim]
        return lax.rem(mine[dim] + offset + size, size)

    def middle(self, first):
        dims = list(range(1, self.core))
        first = first % max(len(dims), 1)
        return dims[first:] + dims[:first]


def greet(grid, row, col, mine):
    barrier = pltpu.get_barrier_semaphore()
    count = 0
    for dim, size in enumerate(grid.sizes):
        for offset in range(1, size):
            pl.semaphore_signal(
                barrier,
                inc=1,
                device_id=grid.partner(row, col, mine, dim, grid.moved(mine, dim, offset)),
                device_id_type=MESH,
            )
            count += 1
    pl.semaphore_wait(barrier, count)


def semaphore_table(grid, orders):
    table, count = {}, 0
    for part, (_, _, order) in enumerate(orders):
        for dim in order:
            for offset in range(1, grid.sizes[dim]):
                table[part, dim, offset] = count
                count += 1
    return table, count


def gather_kernel(grid, orders, table, x_ref, o_ref, send_sem, recv_sem):
    row, col, mine = grid.place()
    greet(grid, row, col, mine)
    o_ref[tuple(mine)] = x_ref[...]
    started = []

    def region(part, step, values):
        first, last, order = orders[part]
        done = order[:step]
        return o_ref.at[
            tuple(slice(None) if d in done else values[d] for d in range(len(values)))
            + (pl.ds(first, last - first),)
        ]

    def start(part, step):
        dim = orders[part][2][step]
        source = region(part, step, mine)
        for offset in range(1, grid.sizes[dim]):
            sem = table[part, dim, offset]
            copy = pltpu.make_async_remote_copy(
                src_ref=source,
                dst_ref=source,
                send_sem=send_sem.at[sem],
                recv_sem=recv_sem.at[sem],
                device_id=grid.partner(row, col, mine, dim, grid.moved(mine, dim, offset)),
                device_id_type=MESH,
            )
            copy.start()
            started.append(copy)

    def finish(part, step):
        dim = orders[part][2][step]
        for offset in range(1, grid.sizes[dim]):
            sem = table[part, dim, offset]
            theirs = list(mine)
            theirs[dim] = grid.moved(mine, dim, -offset)
            landing = region(part, step, theirs)
            pltpu.make_async_remote_copy(
                src_ref=landing,
                dst_ref=landing,
                send_sem=send_sem.at[sem],
                recv_sem=recv_sem.at[sem],
                device_id=grid.partner(row, col, mine, dim, theirs[dim]),
                device_id_type=MESH,
            ).wait_recv()

    for part in range(len(orders)):
        start(part, 0)
    steps = len(grid.sizes)
    for step in range(steps):
        for part in range(len(orders)):
            finish(part, step)
            if step + 1 < steps:
                start(part, step + 1)
    for copy in started:
        copy.wait_send()


def gather(grid, x, cuts, collective_id):
    rows, cols = x.shape
    orders = []
    for part, (first, last) in enumerate(zip(cuts[:-1], cuts[1:])):
        orders.append((first, last, [0] + grid.middle(part) + [grid.core]))
    table, count = semaphore_table(grid, orders)
    out = pl.pallas_call(
        functools.partial(gather_kernel, grid, orders, table),
        out_shape=jax.ShapeDtypeStruct(tuple(grid.sizes) + (rows, cols), x.dtype),
        in_specs=[pl.BlockSpec(memory_space=pltpu.VMEM)],
        out_specs=pl.BlockSpec(memory_space=pltpu.VMEM),
        scratch_shapes=[pltpu.SemaphoreType.DMA((count,)), pltpu.SemaphoreType.DMA((count,))],
        compiler_params=pltpu.CompilerParams(
            collective_id=collective_id, has_side_effects=True, vmem_limit_bytes=LIMIT
        ),
    )(x)
    return out.reshape(grid.n_row * grid.n_col, rows, cols)


def reduce_kernel(grid, orders, table, produce, n_in, *refs):
    ins, out_ref = refs[:n_in], refs[n_in]
    total, core_out, core_in = refs[n_in + 1 : n_in + 4]
    core_send, core_recv, send_sem, recv_sem = refs[n_in + 4 : n_in + 8]
    n_parts = len(orders)
    outgoing = refs[n_in + 8 : n_in + 8 + len(table)]
    incoming = refs[n_in + 8 + len(table) :]
    row, col, mine = grid.place()
    greet(grid, row, col, mine)
    core = grid.core
    other = 1 - mine[core]
    between = (slice(None),) * (core - 1)
    shape = total.shape[1:]
    core_copies = []
    for z in range(grid.n_row):
        total[z] = produce(z, *ins).reshape(shape)
        core_out[z] = total[(z,) + between + (other,)].astype(jnp.bfloat16)
        copy = pltpu.make_async_remote_copy(
            src_ref=core_out.at[z],
            dst_ref=core_in.at[z],
            send_sem=core_send.at[z],
            recv_sem=core_recv.at[z],
            device_id=grid.partner(row, col, mine, core, other),
            device_id_type=MESH,
        )
        copy.start()
        core_copies.append(copy)
    for z, copy in enumerate(core_copies):
        copy.wait_recv()
        where = (z,) + between + (mine[core],)
        total[where] = total[where] + core_in[z].astype(jnp.float32)

    started = []

    def region(part, step, value):
        first, last, order = orders[part]
        dim, done = order[step], order[:step]
        index = []
        for d in range(core):
            index.append(value if d == dim else mine[d] if d in done else slice(None))
        return tuple(index) + (mine[core], pl.ds(first, last - first))

    def start(part, step):
        dim = orders[part][2][step]
        for offset in range(1, grid.sizes[dim]):
            sem = table[part, dim, offset]
            value = grid.moved(mine, dim, offset)
            outgoing[sem][...] = total[region(part, step, value)].astype(jnp.bfloat16)
            copy = pltpu.make_async_remote_copy(
                src_ref=outgoing[sem],
                dst_ref=incoming[sem],
                send_sem=send_sem.at[sem],
                recv_sem=recv_sem.at[sem],
                device_id=grid.partner(row, col, mine, dim, value),
                device_id_type=MESH,
            )
            copy.start()
            started.append(copy)
            waiting[part, step, offset] = copy

    def finish(part, step):
        dim = orders[part][2][step]
        where = region(part, step, mine[dim])
        value = total[where]
        for offset in range(1, grid.sizes[dim]):
            waiting[part, step, offset].wait_recv()
            value = value + incoming[table[part, dim, offset]][...].astype(jnp.float32)
        total[where] = value

    waiting = {}
    for part in range(n_parts):
        start(part, 0)
    steps = core
    turns = []
    for part in range(n_parts):
        late = 1.5 if orders[part][2][0] == 0 else 0
        for step in range(steps):
            turns.append((step + late, part, step))
    for _, part, step in sorted(turns):
        finish(part, step)
        if step + 1 < steps:
            start(part, step + 1)
    out_ref[...] = total[tuple(mine)]
    for copy in core_copies + started:
        copy.wait_send()


def reduce_scatter(grid, produce, ins, rows, cols, plan, collective_id):
    core = grid.core
    orders = []
    for first, last, turn, row_first in plan:
        middle = grid.middle(turn)
        orders.append((first, last, [0] + middle if row_first else middle + [0]))
    table, count = semaphore_table(grid, orders)
    buffers = []
    for part, (first, last, order) in enumerate(orders):
        for step, dim in enumerate(order):
            left = tuple(grid.sizes[d] for d in range(core) if d not in order[: step + 1])
            for offset in range(1, grid.sizes[dim]):
                buffers.append(pltpu.VMEM(left + (last - first, cols), jnp.bfloat16))
    sizes = tuple(grid.sizes)
    half = pltpu.VMEM(sizes[:-1] + (rows, cols), jnp.bfloat16)
    return pl.pallas_call(
        functools.partial(reduce_kernel, grid, orders, table, produce, len(ins)),
        out_shape=jax.ShapeDtypeStruct((rows, cols), jnp.float32),
        in_specs=[pl.BlockSpec(memory_space=pltpu.VMEM)] * len(ins),
        out_specs=pl.BlockSpec(memory_space=pltpu.VMEM),
        scratch_shapes=[
            pltpu.VMEM(sizes + (rows, cols), jnp.float32),
            half,
            half,
            pltpu.SemaphoreType.DMA((grid.n_row,)),
            pltpu.SemaphoreType.DMA((grid.n_row,)),
            pltpu.SemaphoreType.DMA((count,)),
            pltpu.SemaphoreType.DMA((count,)),
        ]
        + buffers
        + buffers,
        compiler_params=pltpu.CompilerParams(
            collective_id=collective_id, has_side_effects=True, vmem_limit_bytes=LIMIT
        ),
    )(*ins)


def contract_first(left, right):
    return lax.dot_general(
        left, right, (((0,), (0,)), ((), ())), preferred_element_type=jnp.float32
    )


def query_slab(z, height, dscores_ref, pa_ref):
    return jnp.dot(
        dscores_ref[z * height : (z + 1) * height, :],
        pa_ref[...],
        preferred_element_type=jnp.float32,
    )


def adapter_slab(z, width, passages_ref, dpa_ref, queries_ref, dqa_ref):
    columns = slice(z * width, (z + 1) * width)
    return contract_first(passages_ref[:, columns], dpa_ref[...]) + contract_first(
        queries_ref[:, columns], dqa_ref[...]
    )


def thirds(rows):
    unit = rows // 16
    large = (unit * 3) // 8
    if large == 0:
        half = (unit // 2) * 16
        if half == 0:
            return [(0, rows, 0, False)]
        return [(0, half, 0, False), (half, rows, 1, False)]
    return [
        (0, 16 * large, 0, False),
        (16 * large, 32 * large, 1, False),
        (32 * large, rows, 0, True),
    ]


def per_device(grid, queries, passages, adapter, positives):
    scale = adapter.shape[1] ** (-0.5)
    slab_rows = passages.shape[0]
    own_rows, width = queries.shape
    emb = adapter.shape[1]
    n = grid.n_row * grid.n_col
    n_query = own_rows * n
    here = lax.axis_index(("row", "col"))
    local_qa = jnp.dot(queries, adapter, preferred_element_type=jnp.float32).astype(jnp.bfloat16)
    pa = jnp.dot(passages, adapter, preferred_element_type=jnp.float32).astype(jnp.bfloat16)
    cuts = [0, own_rows // 2, own_rows] if own_rows % 32 == 0 else [0, own_rows]
    qa = gather(grid, local_qa, cuts, 0).reshape(n_query, emb)
    scores = (
        lax.dot_general(qa, pa, (((1,), (1,)), ((), ())), preferred_element_type=jnp.float32)
        * scale
    )
    columns = here * slab_rows + jnp.arange(slab_rows, dtype=jnp.int32)
    hit = positives[:, None] == columns[None, :]
    local_max = jnp.max(scores, axis=1)
    local_pos = jnp.sum(jnp.where(hit, scores, 0.0), axis=1)
    local_sum = jnp.sum(jnp.exp(scores - local_max[:, None]), axis=1)
    stats = jnp.stack([local_max, local_sum, local_pos]).reshape(-1, 128)
    stats = gather(grid, stats, [0, 8, stats.shape[0]], 1).reshape(n, 3, n_query)
    top = jnp.max(stats[:, 0], axis=0)
    total = jnp.sum(stats[:, 1] * jnp.exp(stats[:, 0] - top), axis=0)
    picked = jnp.sum(stats[:, 2], axis=0)
    lse = top + jnp.log(total)
    probs = jnp.exp(scores - lse[:, None])
    dscores = ((probs - hit.astype(jnp.float32)) * scale).astype(jnp.bfloat16)
    dqa_own = reduce_scatter(
        grid,
        lambda z, *refs: query_slab(z, n_query // grid.n_row, *refs),
        (dscores, pa),
        own_rows,
        emb,
        thirds(own_rows),
        2,
    ).astype(jnp.bfloat16)
    dpa = contract_first(dscores, qa).astype(jnp.bfloat16)
    query_grad = lax.dot_general(
        dqa_own, adapter, (((1,), (1,)), ((), ())), preferred_element_type=jnp.float32
    ).astype(jnp.bfloat16)
    adapter_grad = reduce_scatter(
        grid,
        lambda z, *refs: adapter_slab(z, width // grid.n_row, *refs),
        (passages, dpa, queries, dqa_own),
        width // n,
        emb,
        thirds(width // n),
        3,
    )
    first_row = here * own_rows
    losses = lax.dynamic_slice_in_dim(lse - picked, first_row, own_rows, 0)
    return (adapter_grad, query_grad, losses)


def solution(mesh):
    grid = Grid(mesh.shape["row"], mesh.shape["col"])
    placed = (P(("row", "col"), None), P(("row", "col"), None), P(), P())
    return jax.shard_map(
        functools.partial(per_device, grid),
        mesh=mesh,
        in_specs=placed,
        out_specs=(P(("row", "col"), None), P(("row", "col"), None), P(("row", "col"))),
        check_vma=False,
    )
```

```python
import functools

import jax
import jax.numpy as jnp
from jax import lax
from jax.experimental import pallas as pl
from jax.experimental.pallas import tpu as pltpu
from jax.sharding import PartitionSpec as P

MESH = pl.DeviceIdType.MESH
LIMIT = 56 * 1024 * 1024


class Grid:
    def __init__(self, n_row, n_col):
        factors, left = [], n_col
        while left % 2 == 0:
            factors.append(2)
            left //= 2
        if left > 1:
            factors.insert(0, left)
        self.sizes = [n_row] + factors[::-1] if left == 1 else [n_row] + factors
        self.n_row, self.n_col = n_row, n_col
        self.core = len(self.sizes) - 1
        self.strides = [0] * len(self.sizes)
        stride = 1
        for dim in range(self.core, 0, -1):
            self.strides[dim] = stride
            stride *= self.sizes[dim]

    def place(self):
        row, col = lax.axis_index("row"), lax.axis_index("col")
        mine = [row]
        for dim in range(1, self.core + 1):
            mine.append(lax.rem(col // self.strides[dim], self.sizes[dim]))
        return row, col, mine

    def partner(self, row, col, mine, dim, value):
        if dim == 0:
            return (value, col)
        return (row, col + (value - mine[dim]) * self.strides[dim])

    def moved(self, mine, dim, offset):
        size = self.sizes[dim]
        return lax.rem(mine[dim] + offset + size, size)

    def middle(self, first):
        dims = list(range(1, self.core))
        first = first % max(len(dims), 1)
        return dims[first:] + dims[:first]


def greet(grid, row, col, mine):
    barrier = pltpu.get_barrier_semaphore()
    count = 0
    for dim, size in enumerate(grid.sizes):
        for offset in range(1, size):
            pl.semaphore_signal(
                barrier,
                inc=1,
                device_id=grid.partner(row, col, mine, dim, grid.moved(mine, dim, offset)),
                device_id_type=MESH,
            )
            count += 1
    pl.semaphore_wait(barrier, count)


def semaphore_table(grid, orders):
    table, count = {}, 0
    for part, (_, _, order) in enumerate(orders):
        for dim in order:
            for offset in range(1, grid.sizes[dim]):
                table[part, dim, offset] = count
                count += 1
    return table, count


def gather_kernel(grid, orders, table, beside, n_extra, x_ref, *refs):
    extra, o_ref, beside_ref = refs[:n_extra], refs[n_extra], refs[n_extra + 1]
    send_sem, recv_sem = refs[n_extra + 2 :]
    row, col, mine = grid.place()
    greet(grid, row, col, mine)
    o_ref[tuple(mine)] = x_ref[...]
    started = []

    def region(part, step, values):
        first, last, order = orders[part]
        done = order[:step]
        return o_ref.at[
            tuple(slice(None) if d in done else values[d] for d in range(len(values)))
            + (pl.ds(first, last - first),)
        ]

    def start(part, step):
        dim = orders[part][2][step]
        source = region(part, step, mine)
        for offset in range(1, grid.sizes[dim]):
            sem = table[part, dim, offset]
            copy = pltpu.make_async_remote_copy(
                src_ref=source,
                dst_ref=source,
                send_sem=send_sem.at[sem],
                recv_sem=recv_sem.at[sem],
                device_id=grid.partner(row, col, mine, dim, grid.moved(mine, dim, offset)),
                device_id_type=MESH,
            )
            copy.start()
            started.append(copy)

    def finish(part, step):
        dim = orders[part][2][step]
        for offset in range(1, grid.sizes[dim]):
            sem = table[part, dim, offset]
            theirs = list(mine)
            theirs[dim] = grid.moved(mine, dim, -offset)
            landing = region(part, step, theirs)
            pltpu.make_async_remote_copy(
                src_ref=landing,
                dst_ref=landing,
                send_sem=send_sem.at[sem],
                recv_sem=recv_sem.at[sem],
                device_id=grid.partner(row, col, mine, dim, theirs[dim]),
                device_id_type=MESH,
            ).wait_recv()

    for part in range(len(orders)):
        start(part, 0)
    beside(*extra, beside_ref)
    steps = len(grid.sizes)
    for step in range(steps):
        for part in range(len(orders)):
            finish(part, step)
            if step + 1 < steps:
                start(part, step + 1)
    for copy in started:
        copy.wait_send()


def gather(grid, x, cuts, beside, extra, beside_shape, collective_id):
    rows, cols = x.shape
    orders = []
    for part, (first, last) in enumerate(zip(cuts[:-1], cuts[1:])):
        orders.append((first, last, [0] + grid.middle(part) + [grid.core]))
    table, count = semaphore_table(grid, orders)
    out, made = pl.pallas_call(
        functools.partial(gather_kernel, grid, orders, table, beside, len(extra)),
        out_shape=(
            jax.ShapeDtypeStruct(tuple(grid.sizes) + (rows, cols), x.dtype),
            jax.ShapeDtypeStruct(beside_shape, jnp.bfloat16),
        ),
        in_specs=[pl.BlockSpec(memory_space=pltpu.VMEM)] * (1 + len(extra)),
        out_specs=[pl.BlockSpec(memory_space=pltpu.VMEM)] * 2,
        scratch_shapes=[pltpu.SemaphoreType.DMA((count,)), pltpu.SemaphoreType.DMA((count,))],
        compiler_params=pltpu.CompilerParams(
            collective_id=collective_id, has_side_effects=True, vmem_limit_bytes=LIMIT
        ),
    )(x, *extra)
    return out.reshape(grid.n_row * grid.n_col * rows, cols), made


def stats_kernel(grid, dims, x_ref, o_ref, state, incoming, send_sem, recv_sem):
    row, col, mine = grid.place()
    greet(grid, row, col, mine)
    started, slot = [], 0
    top, total, picked = x_ref[0], x_ref[1], x_ref[2]
    for step, dim in enumerate(dims):
        state[step, 0], state[step, 1], state[step, 2] = top, total, picked
        copies = []
        for offset in range(1, grid.sizes[dim]):
            copy = pltpu.make_async_remote_copy(
                src_ref=state.at[step],
                dst_ref=incoming.at[slot],
                send_sem=send_sem.at[slot],
                recv_sem=recv_sem.at[slot],
                device_id=grid.partner(row, col, mine, dim, grid.moved(mine, dim, offset)),
                device_id_type=MESH,
            )
            copy.start()
            copies.append((slot, copy))
            slot += 1
        for at, copy in copies:
            copy.wait_recv()
            theirs = incoming[at, 0]
            higher = jnp.maximum(top, theirs)
            total = total * jnp.exp(top - higher) + incoming[at, 1] * jnp.exp(theirs - higher)
            picked = picked + incoming[at, 2]
            top = higher
            started.append(copy)
    o_ref[0] = top + jnp.log(total)
    o_ref[1] = picked
    for copy in started:
        copy.wait_send()


def combine_stats(grid, stats, collective_id):
    dims = list(range(grid.core, -1, -1))
    slots = sum(size - 1 for size in grid.sizes)
    return pl.pallas_call(
        functools.partial(stats_kernel, grid, dims),
        out_shape=jax.ShapeDtypeStruct((2,) + stats.shape[1:], jnp.float32),
        in_specs=[pl.BlockSpec(memory_space=pltpu.VMEM)],
        out_specs=pl.BlockSpec(memory_space=pltpu.VMEM),
        scratch_shapes=[
            pltpu.VMEM((len(dims),) + stats.shape, jnp.float32),
            pltpu.VMEM((slots,) + stats.shape, jnp.float32),
            pltpu.SemaphoreType.DMA((slots,)),
            pltpu.SemaphoreType.DMA((slots,)),
        ],
        compiler_params=pltpu.CompilerParams(collective_id=collective_id, has_side_effects=True),
    )(stats)


def reduce_kernel(grid, orders, table, produce, beside, n_in, n_extra, *refs):
    ins, extra = refs[:n_in], refs[n_in : n_in + n_extra]
    refs = refs[n_in + n_extra :]
    out_ref, beside_ref, total, core_out, core_in = refs[:5]
    core_send, core_recv, send_sem, recv_sem = refs[5:9]
    outgoing, incoming = refs[9 : 9 + len(table)], refs[9 + len(table) :]
    row, col, mine = grid.place()
    greet(grid, row, col, mine)
    core, n_row = grid.core, grid.n_row
    other = 1 - mine[core]
    between = (slice(None),) * (core - 1)
    shape = total.shape[1:]
    slabs = [grid.moved(mine, 0, turn + 1) for turn in range(n_row)]
    started, waiting = [], {}

    def region(part, step, value):
        first, last, order = orders[part]
        dim, done = order[step], order[:step]
        index = []
        for d in range(core):
            index.append(value if d == dim else mine[d] if d in done else slice(None))
        return tuple(index) + (mine[core], pl.ds(first, last - first))

    def send(part, step, offset, turn=None):
        dim = orders[part][2][step]
        entry = table[part, dim, offset]
        value = grid.moved(mine, dim, offset)
        where = region(part, step, value)
        source, target, sem = outgoing[entry], incoming[entry], entry * n_row
        if turn is not None:
            where = (slabs[turn],) + where[1:]
            source, target, sem = source.at[turn], target.at[turn], sem + turn
        source[...] = total[where].astype(jnp.bfloat16)
        copy = pltpu.make_async_remote_copy(
            src_ref=source,
            dst_ref=target,
            send_sem=send_sem.at[sem],
            recv_sem=recv_sem.at[sem],
            device_id=grid.partner(row, col, mine, dim, value),
            device_id_type=MESH,
        )
        copy.start()
        started.append(copy)
        waiting[part, step, offset, turn] = copy

    def core_start(turn):
        z = slabs[turn]
        total[z] = produce(z, *ins).reshape(shape)
        core_out[turn] = total[(z,) + between + (other,)].astype(jnp.bfloat16)
        copy = pltpu.make_async_remote_copy(
            src_ref=core_out.at[turn],
            dst_ref=core_in.at[turn],
            send_sem=core_send.at[turn],
            recv_sem=core_recv.at[turn],
            device_id=grid.partner(row, col, mine, core, other),
            device_id_type=MESH,
        )
        copy.start()
        started.append(copy)
        waiting[turn] = copy

    def core_finish(turn):
        waiting[turn].wait_recv()
        where = (slabs[turn],) + between + (mine[core],)
        total[where] = total[where] + core_in[turn].astype(jnp.float32)
        for part, (_, _, order) in enumerate(orders):
            if order[0] != 0:
                for offset in range(1, grid.sizes[order[0]]):
                    send(part, 0, offset, turn)
            elif turn + 1 < n_row:
                send(part, 0, turn + 1)

    def finish(part, step):
        dim = orders[part][2][step]
        split = step == 0 and dim != 0
        for turn in range(n_row) if split else (None,):
            where = region(part, step, mine[dim])
            if split:
                where = (slabs[turn],) + where[1:]
            value = total[where]
            for offset in range(1, grid.sizes[dim]):
                waiting[part, step, offset, turn].wait_recv()
                landed = incoming[table[part, dim, offset]]
                landed = landed[turn] if split else landed[...]
                value = value + landed.astype(jnp.float32)
            total[where] = value

    for turn in range(n_row):
        core_start(turn)
        if turn:
            core_finish(turn - 1)
    core_finish(n_row - 1)
    beside(*extra, beside_ref)
    steps = core
    turns = []
    for part in range(len(orders)):
        late = 1.5 if orders[part][2][0] == 0 else 0
        for step in range(steps):
            turns.append((step + late, part, step))
    for _, part, step in sorted(turns):
        finish(part, step)
        if step + 1 < steps:
            dim = orders[part][2][step + 1]
            for offset in range(1, grid.sizes[dim]):
                send(part, step + 1, offset)
    out_ref[...] = total[tuple(mine)]
    for copy in started:
        copy.wait_send()


def reduce_scatter(grid, produce, ins, beside, extra, beside_shape, rows, cols, plan, collective_id):
    core = grid.core
    orders = []
    for first, last, turn, row_first in plan:
        middle = grid.middle(turn)
        orders.append((first, last, [0] + middle if row_first else middle + [0]))
    table, count = semaphore_table(grid, orders)
    buffers = []
    for part, (first, last, order) in enumerate(orders):
        for step, dim in enumerate(order):
            left = tuple(grid.sizes[d] for d in range(core) if d not in order[: step + 1])
            for offset in range(1, grid.sizes[dim]):
                buffers.append(pltpu.VMEM(left + (last - first, cols), jnp.bfloat16))
    sizes = tuple(grid.sizes)
    half = pltpu.VMEM(sizes[:-1] + (rows, cols), jnp.bfloat16)
    return pl.pallas_call(
        functools.partial(
            reduce_kernel, grid, orders, table, produce, beside, len(ins), len(extra)
        ),
        out_shape=(
            jax.ShapeDtypeStruct((rows, cols), jnp.float32),
            jax.ShapeDtypeStruct(beside_shape, jnp.bfloat16),
        ),
        in_specs=[pl.BlockSpec(memory_space=pltpu.VMEM)] * (len(ins) + len(extra)),
        out_specs=[pl.BlockSpec(memory_space=pltpu.VMEM)] * 2,
        scratch_shapes=[
            pltpu.VMEM(sizes + (rows, cols), jnp.float32),
            half,
            half,
            pltpu.SemaphoreType.DMA((grid.n_row,)),
            pltpu.SemaphoreType.DMA((grid.n_row,)),
            pltpu.SemaphoreType.DMA((count * grid.n_row,)),
            pltpu.SemaphoreType.DMA((count * grid.n_row,)),
        ]
        + buffers
        + buffers,
        compiler_params=pltpu.CompilerParams(
            collective_id=collective_id, has_side_effects=True, vmem_limit_bytes=LIMIT
        ),
    )(*ins, *extra)


def contract_first(left, right):
    return lax.dot_general(
        left, right, (((0,), (0,)), ((), ())), preferred_element_type=jnp.float32
    )


def query_slab(z, height, dscores_ref, pa_ref):
    return jnp.dot(
        dscores_ref[pl.ds(pl.multiple_of(z * height, height), height), :],
        pa_ref[...],
        preferred_element_type=jnp.float32,
    )


def adapter_slab(z, width, passages_ref, dpa_ref, queries_ref, dqa_ref):
    columns = pl.ds(pl.multiple_of(z * width, width), width)
    return contract_first(passages_ref[:, columns], dpa_ref[...]) + contract_first(
        queries_ref[:, columns], dqa_ref[...]
    )


def adapt(passages_ref, adapter_ref, pa_ref):
    block = min(256, pa_ref.shape[0])

    @pl.loop(0, pa_ref.shape[0] // block)
    def _(step):
        rows = pl.ds(pl.multiple_of(step * block, block), block)
        pa_ref[rows, :] = jnp.dot(
            passages_ref[rows, :], adapter_ref[...], preferred_element_type=jnp.float32
        ).astype(jnp.bfloat16)


def passage_grad(dscores_ref, qa_ref, dpa_ref):
    block = min(256, dpa_ref.shape[0])

    @pl.loop(0, dpa_ref.shape[0] // block)
    def _(step):
        rows = pl.ds(pl.multiple_of(step * block, block), block)
        dpa_ref[rows, :] = contract_first(dscores_ref[:, rows], qa_ref[...]).astype(jnp.bfloat16)


def query_back(dqa_ref, adapter_ref, grad_ref):
    block = min(512, grad_ref.shape[1])

    @pl.loop(0, grad_ref.shape[1] // block)
    def _(step):
        columns = pl.ds(pl.multiple_of(step * block, block), block)
        grad_ref[:, columns] = lax.dot_general(
            dqa_ref[...],
            adapter_ref[columns, :],
            (((1,), (1,)), ((), ())),
            preferred_element_type=jnp.float32,
        ).astype(jnp.bfloat16)


def thirds(rows):
    unit = rows // 16
    large = (unit * 3) // 8
    if large == 0:
        half = (unit // 2) * 16
        if half == 0:
            return [(0, rows, 0, False)]
        return [(0, half, 0, False), (half, rows, 1, False)]
    return [
        (0, 16 * large, 0, False),
        (16 * large, 32 * large, 1, False),
        (32 * large, rows, 0, True),
    ]


def per_device(grid, queries, passages, adapter, positives):
    scale = adapter.shape[1] ** (-0.5)
    slab_rows = passages.shape[0]
    own_rows, width = queries.shape
    emb = adapter.shape[1]
    n = grid.n_row * grid.n_col
    n_query = own_rows * n
    here = lax.axis_index(("row", "col"))
    local_qa = jnp.dot(queries, adapter, preferred_element_type=jnp.float32).astype(jnp.bfloat16)
    cuts = [0, own_rows // 2, own_rows] if own_rows % 32 == 0 else [0, own_rows]
    qa, pa = gather(grid, local_qa, cuts, adapt, (passages, adapter), (slab_rows, emb), 0)
    scores = (
        lax.dot_general(qa, pa, (((1,), (1,)), ((), ())), preferred_element_type=jnp.float32)
        * scale
    )
    columns = here * slab_rows + jnp.arange(slab_rows, dtype=jnp.int32)
    hit = positives[:, None] == columns[None, :]
    local_max = jnp.max(scores, axis=1)
    local_pos = jnp.sum(jnp.where(hit, scores, 0.0), axis=1)
    local_sum = jnp.sum(jnp.exp(scores - local_max[:, None]), axis=1)
    stats = jnp.stack([local_max, local_sum, local_pos]).reshape(3, -1, 128)
    lse, picked = combine_stats(grid, stats, 1).reshape(2, n_query)
    probs = jnp.exp(scores - lse[:, None])
    dscores = ((probs - hit.astype(jnp.float32)) * scale).astype(jnp.bfloat16)
    dqa_own, dpa = reduce_scatter(
        grid,
        lambda z, *refs: query_slab(z, n_query // grid.n_row, *refs),
        (dscores, pa),
        lambda qa_ref, dscores_ref, dpa_ref: passage_grad(dscores_ref, qa_ref, dpa_ref),
        (qa, dscores),
        (slab_rows, emb),
        own_rows,
        emb,
        thirds(own_rows),
        2,
    )
    dqa_own = dqa_own.astype(jnp.bfloat16)
    adapter_grad, query_grad = reduce_scatter(
        grid,
        lambda z, *refs: adapter_slab(z, width // grid.n_row, *refs),
        (passages, dpa, queries, dqa_own),
        query_back,
        (dqa_own, adapter),
        (own_rows, width),
        width // n,
        emb,
        thirds(width // n),
        3,
    )
    first_row = here * own_rows
    losses = lax.dynamic_slice_in_dim(lse - picked, first_row, own_rows, 0)
    return (adapter_grad, query_grad, losses)


def solution(mesh):
    grid = Grid(mesh.shape["row"], mesh.shape["col"])
    placed = (P(("row", "col"), None), P(("row", "col"), None), P(), P())
    return jax.shard_map(
        functools.partial(per_device, grid),
        mesh=mesh,
        in_specs=placed,
        out_specs=(P(("row", "col"), None), P(("row", "col"), None), P(("row", "col"))),
        check_vma=False,
    )
```

```python
import functools

import jax
import jax.numpy as jnp
from jax import lax
from jax.experimental import pallas as pl
from jax.experimental.pallas import tpu as pltpu
from jax.sharding import PartitionSpec as P

MESH = pl.DeviceIdType.MESH
LIMIT = 56 * 1024 * 1024


class Grid:
    def __init__(self, n_row, n_col):
        factors, left = [], n_col
        while left % 2 == 0:
            factors.append(2)
            left //= 2
        if left > 1:
            factors.insert(0, left)
        self.sizes = [n_row] + factors[::-1] if left == 1 else [n_row] + factors
        self.n_row, self.n_col = n_row, n_col
        self.core = len(self.sizes) - 1
        self.strides = [0] * len(self.sizes)
        stride = 1
        for dim in range(self.core, 0, -1):
            self.strides[dim] = stride
            stride *= self.sizes[dim]

    def place(self):
        row, col = lax.axis_index("row"), lax.axis_index("col")
        mine = [row]
        for dim in range(1, self.core + 1):
            mine.append(lax.rem(col // self.strides[dim], self.sizes[dim]))
        return row, col, mine

    def partner(self, row, col, mine, dim, value):
        if dim == 0:
            return (value, col)
        return (row, col + (value - mine[dim]) * self.strides[dim])

    def moved(self, mine, dim, offset):
        size = self.sizes[dim]
        return lax.rem(mine[dim] + offset + size, size)

    def middle(self, first):
        dims = list(range(1, self.core))
        first = first % max(len(dims), 1)
        return dims[first:] + dims[:first]


def greet(grid, row, col, mine):
    barrier = pltpu.get_barrier_semaphore()
    count = 0
    for dim, size in enumerate(grid.sizes):
        for offset in range(1, size):
            pl.semaphore_signal(
                barrier,
                inc=1,
                device_id=grid.partner(row, col, mine, dim, grid.moved(mine, dim, offset)),
                device_id_type=MESH,
            )
            count += 1
    pl.semaphore_wait(barrier, count)


def semaphore_table(grid, orders):
    table, count = {}, 0
    for part, (_, _, order) in enumerate(orders):
        for dim in order:
            for offset in range(1, grid.sizes[dim]):
                table[part, dim, offset] = count
                count += 1
    return table, count


def gather_kernel(grid, orders, table, beside, n_extra, x_ref, *refs):
    extra, o_ref, beside_ref = refs[:n_extra], refs[n_extra], refs[n_extra + 1]
    send_sem, recv_sem = refs[n_extra + 2 :]
    row, col, mine = grid.place()
    greet(grid, row, col, mine)
    o_ref[tuple(mine)] = x_ref[...]
    started = []

    def region(part, step, values):
        first, last, order = orders[part]
        done = order[:step]
        return o_ref.at[
            tuple(slice(None) if d in done else values[d] for d in range(len(values)))
            + (pl.ds(first, last - first),)
        ]

    def start(part, step):
        dim = orders[part][2][step]
        source = region(part, step, mine)
        for offset in range(1, grid.sizes[dim]):
            sem = table[part, dim, offset]
            copy = pltpu.make_async_remote_copy(
                src_ref=source,
                dst_ref=source,
                send_sem=send_sem.at[sem],
                recv_sem=recv_sem.at[sem],
                device_id=grid.partner(row, col, mine, dim, grid.moved(mine, dim, offset)),
                device_id_type=MESH,
            )
            copy.start()
            started.append(copy)

    def finish(part, step):
        dim = orders[part][2][step]
        for offset in range(1, grid.sizes[dim]):
            sem = table[part, dim, offset]
            theirs = list(mine)
            theirs[dim] = grid.moved(mine, dim, -offset)
            landing = region(part, step, theirs)
            pltpu.make_async_remote_copy(
                src_ref=landing,
                dst_ref=landing,
                send_sem=send_sem.at[sem],
                recv_sem=recv_sem.at[sem],
                device_id=grid.partner(row, col, mine, dim, theirs[dim]),
                device_id_type=MESH,
            ).wait_recv()

    for part in range(len(orders)):
        start(part, 0)
    beside(0, *extra, beside_ref)
    steps = len(grid.sizes)
    for step in range(steps):
        for part in range(len(orders)):
            finish(part, step)
            if step + 1 < steps:
                start(part, step + 1)
        if step + 1 < steps:
            beside(step + 1, *extra, beside_ref)
    for copy in started:
        copy.wait_send()


def gather(grid, x, cuts, beside, extra, beside_shape, collective_id):
    rows, cols = x.shape
    orders = []
    for part, (first, last) in enumerate(zip(cuts[:-1], cuts[1:])):
        orders.append((first, last, [0] + grid.middle(part) + [grid.core]))
    table, count = semaphore_table(grid, orders)
    out, made = pl.pallas_call(
        functools.partial(gather_kernel, grid, orders, table, beside, len(extra)),
        out_shape=(
            jax.ShapeDtypeStruct(tuple(grid.sizes) + (rows, cols), x.dtype),
            jax.ShapeDtypeStruct(beside_shape, jnp.bfloat16),
        ),
        in_specs=[pl.BlockSpec(memory_space=pltpu.VMEM)] * (1 + len(extra)),
        out_specs=[pl.BlockSpec(memory_space=pltpu.VMEM)] * 2,
        scratch_shapes=[pltpu.SemaphoreType.DMA((count,)), pltpu.SemaphoreType.DMA((count,))],
        compiler_params=pltpu.CompilerParams(
            collective_id=collective_id, has_side_effects=True, vmem_limit_bytes=LIMIT
        ),
    )(x, *extra)
    return out.reshape(grid.n_row * grid.n_col * rows, cols), made


def stats_kernel(grid, dims, x_ref, o_ref, state, incoming, send_sem, recv_sem):
    row, col, mine = grid.place()
    greet(grid, row, col, mine)
    started, slot = [], 0
    top, total, picked = x_ref[0], x_ref[1], x_ref[2]
    for step, dim in enumerate(dims):
        state[step, 0], state[step, 1], state[step, 2] = top, total, picked
        copies = []
        for offset in range(1, grid.sizes[dim]):
            copy = pltpu.make_async_remote_copy(
                src_ref=state.at[step],
                dst_ref=incoming.at[slot],
                send_sem=send_sem.at[slot],
                recv_sem=recv_sem.at[slot],
                device_id=grid.partner(row, col, mine, dim, grid.moved(mine, dim, offset)),
                device_id_type=MESH,
            )
            copy.start()
            copies.append((slot, copy))
            slot += 1
        for at, copy in copies:
            copy.wait_recv()
            theirs = incoming[at, 0]
            higher = jnp.maximum(top, theirs)
            total = total * jnp.exp(top - higher) + incoming[at, 1] * jnp.exp(theirs - higher)
            picked = picked + incoming[at, 2]
            top = higher
            started.append(copy)
    o_ref[0] = top + jnp.log(total)
    o_ref[1] = picked
    for copy in started:
        copy.wait_send()


def combine_stats(grid, stats, collective_id):
    dims = list(range(grid.core, -1, -1))
    slots = sum(size - 1 for size in grid.sizes)
    return pl.pallas_call(
        functools.partial(stats_kernel, grid, dims),
        out_shape=jax.ShapeDtypeStruct((2,) + stats.shape[1:], jnp.float32),
        in_specs=[pl.BlockSpec(memory_space=pltpu.VMEM)],
        out_specs=pl.BlockSpec(memory_space=pltpu.VMEM),
        scratch_shapes=[
            pltpu.VMEM((len(dims),) + stats.shape, jnp.float32),
            pltpu.VMEM((slots,) + stats.shape, jnp.float32),
            pltpu.SemaphoreType.DMA((slots,)),
            pltpu.SemaphoreType.DMA((slots,)),
        ],
        compiler_params=pltpu.CompilerParams(collective_id=collective_id, has_side_effects=True),
    )(stats)


def reduce_kernel(grid, orders, table, produce, beside, n_in, n_extra, *refs):
    ins, extra = refs[:n_in], refs[n_in : n_in + n_extra]
    refs = refs[n_in + n_extra :]
    out_ref, beside_ref, total, core_out, core_in = refs[:5]
    core_send, core_recv, send_sem, recv_sem = refs[5:9]
    outgoing, incoming = refs[9 : 9 + len(table)], refs[9 + len(table) :]
    row, col, mine = grid.place()
    greet(grid, row, col, mine)
    core, n_row = grid.core, grid.n_row
    other = 1 - mine[core]
    between = (slice(None),) * (core - 1)
    shape = total.shape[1:]
    slabs = [grid.moved(mine, 0, turn + 1) for turn in range(n_row)]
    started, waiting = [], {}

    def region(part, step, turn, value):
        first, last, order = orders[part]
        dim, done = order[step], order[:step]
        index = [slabs[turn]]
        for d in range(1, core):
            index.append(value if d == dim else mine[d] if d in done else slice(None))
        return tuple(index) + (mine[core], pl.ds(first, last - first))

    def send(part, step, turn):
        dim = orders[part][2][step]
        offsets = (turn + 1,) if dim == 0 else range(1, grid.sizes[dim])
        for offset in offsets:
            entry = table[part, dim, offset]
            value = grid.moved(mine, dim, offset)
            source, target, sem = outgoing[entry], incoming[entry], entry * n_row
            if dim != 0:
                source, target, sem = source.at[turn], target.at[turn], sem + turn
            source[...] = total[region(part, step, turn, value)].astype(jnp.bfloat16)
            copy = pltpu.make_async_remote_copy(
                src_ref=source,
                dst_ref=target,
                send_sem=send_sem.at[sem],
                recv_sem=recv_sem.at[sem],
                device_id=grid.partner(row, col, mine, dim, value),
                device_id_type=MESH,
            )
            copy.start()
            started.append(copy)
            waiting[part, step, turn, offset] = copy

    def finish(part, step, turn):
        dim = orders[part][2][step]
        where = region(part, step, turn, mine[dim])
        value = total[where]
        for offset in range(1, grid.sizes[dim]):
            waiting[part, step, turn, offset].wait_recv()
            landed = incoming[table[part, dim, offset]][turn]
            value = value + landed.astype(jnp.float32)
        total[where] = value

    def core_start(turn):
        z = slabs[turn]
        total[z] = produce(z, *ins).reshape(shape)
        core_out[turn] = total[(z,) + between + (other,)].astype(jnp.bfloat16)
        copy = pltpu.make_async_remote_copy(
            src_ref=core_out.at[turn],
            dst_ref=core_in.at[turn],
            send_sem=core_send.at[turn],
            recv_sem=core_recv.at[turn],
            device_id=grid.partner(row, col, mine, core, other),
            device_id_type=MESH,
        )
        copy.start()
        started.append(copy)
        waiting[turn] = copy

    def core_finish(turn):
        waiting[turn].wait_recv()
        where = (slabs[turn],) + between + (mine[core],)
        total[where] = total[where] + core_in[turn].astype(jnp.float32)
        for part in range(len(orders)):
            follow(part, 0, turn)

    def follow(part, step, turn):
        if step < core - 1 or turn + 1 < n_row:
            send(part, step, turn)

    for turn in range(n_row):
        core_start(turn)
        if turn:
            core_finish(turn - 1)
    core_finish(n_row - 1)
    beside(*extra, beside_ref)
    turns = [(turn + step, turn, step) for turn in range(n_row) for step in range(core - 1)]
    for _, turn, step in sorted(turns):
        for part in range(len(orders)):
            finish(part, step, turn)
            follow(part, step + 1, turn)
    for part, (first, last, _) in enumerate(orders):
        where = tuple(mine) + (pl.ds(first, last - first),)
        value = total[where]
        for offset in range(1, n_row):
            waiting[part, core - 1, offset - 1, offset].wait_recv()
            value = value + incoming[table[part, 0, offset]][...].astype(jnp.float32)
        out_ref[first:last, :] = value
    for copy in started:
        copy.wait_send()


def reduce_scatter(grid, produce, ins, beside, extra, beside_shape, rows, cols, cuts, collective_id):
    core = grid.core
    orders = []
    for turn, (first, last) in enumerate(zip(cuts[:-1], cuts[1:])):
        orders.append((first, last, grid.middle(turn) + [0]))
    table, count = semaphore_table(grid, orders)
    buffers = []
    for part, (first, last, order) in enumerate(orders):
        for step, dim in enumerate(order):
            left = tuple(grid.sizes[d] for d in range(core) if d not in order[: step + 1])
            for offset in range(1, grid.sizes[dim]):
                buffers.append(pltpu.VMEM(left + (last - first, cols), jnp.bfloat16))
    sizes = tuple(grid.sizes)
    half = pltpu.VMEM(sizes[:-1] + (rows, cols), jnp.bfloat16)
    return pl.pallas_call(
        functools.partial(
            reduce_kernel, grid, orders, table, produce, beside, len(ins), len(extra)
        ),
        out_shape=(
            jax.ShapeDtypeStruct((rows, cols), jnp.float32),
            jax.ShapeDtypeStruct(beside_shape, jnp.bfloat16),
        ),
        in_specs=[pl.BlockSpec(memory_space=pltpu.VMEM)] * (len(ins) + len(extra)),
        out_specs=[pl.BlockSpec(memory_space=pltpu.VMEM)] * 2,
        scratch_shapes=[
            pltpu.VMEM(sizes + (rows, cols), jnp.float32),
            half,
            half,
            pltpu.SemaphoreType.DMA((grid.n_row,)),
            pltpu.SemaphoreType.DMA((grid.n_row,)),
            pltpu.SemaphoreType.DMA((count * grid.n_row,)),
            pltpu.SemaphoreType.DMA((count * grid.n_row,)),
        ]
        + buffers
        + buffers,
        compiler_params=pltpu.CompilerParams(
            collective_id=collective_id, has_side_effects=True, vmem_limit_bytes=LIMIT
        ),
    )(*ins, *extra)


def contract_first(left, right):
    return lax.dot_general(
        left, right, (((0,), (0,)), ((), ())), preferred_element_type=jnp.float32
    )


def query_slab(z, height, dscores_ref, pa_ref):
    return jnp.dot(
        dscores_ref[pl.ds(pl.multiple_of(z * height, height), height), :],
        pa_ref[...],
        preferred_element_type=jnp.float32,
    )


def adapter_slab(z, width, passages_ref, dpa_ref, queries_ref, dqa_ref):
    columns = pl.ds(pl.multiple_of(z * width, width), width)
    return contract_first(passages_ref[:, columns], dpa_ref[...]) + contract_first(
        queries_ref[:, columns], dqa_ref[...]
    )


def adapt(step, passages_ref, adapter_ref, pa_ref):
    block = pa_ref.shape[0] // 2
    if step < 2:
        rows = slice(step * block, (step + 1) * block)
        pa_ref[rows, :] = jnp.dot(
            passages_ref[rows, :], adapter_ref[...], preferred_element_type=jnp.float32
        ).astype(jnp.bfloat16)


def passage_grad(dscores_ref, qa_ref, dpa_ref):
    block = min(256, dpa_ref.shape[0])

    @pl.loop(0, dpa_ref.shape[0] // block)
    def _(step):
        rows = pl.ds(pl.multiple_of(step * block, block), block)
        dpa_ref[rows, :] = contract_first(dscores_ref[:, rows], qa_ref[...]).astype(jnp.bfloat16)


def query_back(dqa_ref, adapter_ref, grad_ref):
    block = min(512, grad_ref.shape[1])

    @pl.loop(0, grad_ref.shape[1] // block)
    def _(step):
        columns = pl.ds(pl.multiple_of(step * block, block), block)
        grad_ref[:, columns] = lax.dot_general(
            dqa_ref[...],
            adapter_ref[columns, :],
            (((1,), (1,)), ((), ())),
            preferred_element_type=jnp.float32,
        ).astype(jnp.bfloat16)


def halves(rows):
    return [0, rows // 2, rows] if rows % 32 == 0 else [0, rows]


def per_device(grid, queries, passages, adapter, positives):
    scale = adapter.shape[1] ** (-0.5)
    slab_rows = passages.shape[0]
    own_rows, width = queries.shape
    emb = adapter.shape[1]
    n = grid.n_row * grid.n_col
    n_query = own_rows * n
    here = lax.axis_index(("row", "col"))
    local_qa = jnp.dot(queries, adapter, preferred_element_type=jnp.float32).astype(jnp.bfloat16)
    qa, pa = gather(grid, local_qa, halves(own_rows), adapt, (passages, adapter), (slab_rows, emb), 0)
    scores = (
        lax.dot_general(qa, pa, (((1,), (1,)), ((), ())), preferred_element_type=jnp.float32)
        * scale
    )
    columns = here * slab_rows + jnp.arange(slab_rows, dtype=jnp.int32)
    hit = positives[:, None] == columns[None, :]
    local_max = jnp.max(scores, axis=1)
    local_pos = jnp.sum(jnp.where(hit, scores, 0.0), axis=1)
    local_sum = jnp.sum(jnp.exp(scores - local_max[:, None]), axis=1)
    stats = jnp.stack([local_max, local_sum, local_pos]).reshape(3, -1, 128)
    lse, picked = combine_stats(grid, stats, 1).reshape(2, n_query)
    probs = jnp.exp(scores - lse[:, None])
    dscores = ((probs - hit.astype(jnp.float32)) * scale).astype(jnp.bfloat16)
    dqa_own, dpa = reduce_scatter(
        grid,
        lambda z, *refs: query_slab(z, n_query // grid.n_row, *refs),
        (dscores, pa),
        lambda qa_ref, dscores_ref, dpa_ref: passage_grad(dscores_ref, qa_ref, dpa_ref),
        (qa, dscores),
        (slab_rows, emb),
        own_rows,
        emb,
        halves(own_rows),
        2,
    )
    dqa_own = dqa_own.astype(jnp.bfloat16)
    adapter_grad, query_grad = reduce_scatter(
        grid,
        lambda z, *refs: adapter_slab(z, width // grid.n_row, *refs),
        (passages, dpa, queries, dqa_own),
        query_back,
        (dqa_own, adapter),
        (own_rows, width),
        width // n,
        emb,
        halves(width // n),
        3,
    )
    first_row = here * own_rows
    losses = lax.dynamic_slice_in_dim(lse - picked, first_row, own_rows, 0)
    return (adapter_grad, query_grad, losses)


def solution(mesh):
    grid = Grid(mesh.shape["row"], mesh.shape["col"])
    placed = (P(("row", "col"), None), P(("row", "col"), None), P(), P())
    return jax.shard_map(
        functools.partial(per_device, grid),
        mesh=mesh,
        in_specs=placed,
        out_specs=(P(("row", "col"), None), P(("row", "col"), None), P(("row", "col"))),
        check_vma=False,
    )
```

```python
import functools

import jax
import jax.numpy as jnp
from jax import lax
from jax.experimental import pallas as pl
from jax.experimental.pallas import tpu as pltpu
from jax.sharding import PartitionSpec as P

MESH = pl.DeviceIdType.MESH
LIMIT = 56 * 1024 * 1024


class Grid:
    def __init__(self, n_row, n_col):
        factors, left = [], n_col
        while left % 2 == 0:
            factors.append(2)
            left //= 2
        if left > 1:
            factors.insert(0, left)
        self.sizes = [n_row] + factors[::-1] if left == 1 else [n_row] + factors
        self.n_row, self.n_col = n_row, n_col
        self.core = len(self.sizes) - 1
        self.strides = [0] * len(self.sizes)
        stride = 1
        for dim in range(self.core, 0, -1):
            self.strides[dim] = stride
            stride *= self.sizes[dim]

    def place(self):
        row, col = lax.axis_index("row"), lax.axis_index("col")
        mine = [row]
        for dim in range(1, self.core + 1):
            mine.append(lax.rem(col // self.strides[dim], self.sizes[dim]))
        return row, col, mine

    def partner(self, row, col, mine, dim, value):
        if dim == 0:
            return (value, col)
        return (row, col + (value - mine[dim]) * self.strides[dim])

    def moved(self, mine, dim, offset):
        size = self.sizes[dim]
        return lax.rem(mine[dim] + offset + size, size)

    def middle(self, first):
        dims = list(range(1, self.core))
        first = first % max(len(dims), 1)
        return dims[first:] + dims[:first]


def greet(grid, row, col, mine):
    barrier = pltpu.get_barrier_semaphore()
    count = 0
    for dim, size in enumerate(grid.sizes):
        for offset in range(1, size):
            pl.semaphore_signal(
                barrier,
                inc=1,
                device_id=grid.partner(row, col, mine, dim, grid.moved(mine, dim, offset)),
                device_id_type=MESH,
            )
            count += 1
    pl.semaphore_wait(barrier, count)


def semaphore_table(grid, orders):
    table, count = {}, 0
    for part, (_, _, order) in enumerate(orders):
        for dim in order:
            for offset in range(1, grid.sizes[dim]):
                table[part, dim, offset] = count
                count += 1
    return table, count


def gather_kernel(grid, orders, table, beside, n_extra, x_ref, *refs):
    extra, o_ref, beside_ref = refs[:n_extra], refs[n_extra], refs[n_extra + 1]
    send_sem, recv_sem = refs[n_extra + 2 :]
    row, col, mine = grid.place()
    greet(grid, row, col, mine)
    o_ref[tuple(mine)] = x_ref[...]
    started = []

    def region(part, step, values):
        first, last, order = orders[part]
        done = order[:step]
        return o_ref.at[
            tuple(slice(None) if d in done else values[d] for d in range(len(values)))
            + (pl.ds(first, last - first),)
        ]

    def start(part, step):
        dim = orders[part][2][step]
        source = region(part, step, mine)
        for offset in range(1, grid.sizes[dim]):
            sem = table[part, dim, offset]
            copy = pltpu.make_async_remote_copy(
                src_ref=source,
                dst_ref=source,
                send_sem=send_sem.at[sem],
                recv_sem=recv_sem.at[sem],
                device_id=grid.partner(row, col, mine, dim, grid.moved(mine, dim, offset)),
                device_id_type=MESH,
            )
            copy.start()
            started.append(copy)

    def finish(part, step):
        dim = orders[part][2][step]
        for offset in range(1, grid.sizes[dim]):
            sem = table[part, dim, offset]
            theirs = list(mine)
            theirs[dim] = grid.moved(mine, dim, -offset)
            landing = region(part, step, theirs)
            pltpu.make_async_remote_copy(
                src_ref=landing,
                dst_ref=landing,
                send_sem=send_sem.at[sem],
                recv_sem=recv_sem.at[sem],
                device_id=grid.partner(row, col, mine, dim, theirs[dim]),
                device_id_type=MESH,
            ).wait_recv()

    for part in range(len(orders)):
        start(part, 0)
    beside(*extra, beside_ref)
    steps = len(grid.sizes)
    for step in range(steps):
        for part in range(len(orders)):
            finish(part, step)
            if step + 1 < steps:
                start(part, step + 1)
    for copy in started:
        copy.wait_send()


def gather(grid, x, cuts, beside, extra, beside_shape, collective_id):
    rows, cols = x.shape
    orders = []
    for part, (first, last) in enumerate(zip(cuts[:-1], cuts[1:])):
        orders.append((first, last, [0] + grid.middle(part) + [grid.core]))
    table, count = semaphore_table(grid, orders)
    out, made = pl.pallas_call(
        functools.partial(gather_kernel, grid, orders, table, beside, len(extra)),
        out_shape=(
            jax.ShapeDtypeStruct(tuple(grid.sizes) + (rows, cols), x.dtype),
            jax.ShapeDtypeStruct(beside_shape, jnp.bfloat16),
        ),
        in_specs=[pl.BlockSpec(memory_space=pltpu.VMEM)] * (1 + len(extra)),
        out_specs=[pl.BlockSpec(memory_space=pltpu.VMEM)] * 2,
        scratch_shapes=[pltpu.SemaphoreType.DMA((count,)), pltpu.SemaphoreType.DMA((count,))],
        compiler_params=pltpu.CompilerParams(
            collective_id=collective_id, has_side_effects=True, vmem_limit_bytes=LIMIT
        ),
    )(x, *extra)
    return out.reshape(grid.n_row * grid.n_col * rows, cols), made


def stats_kernel(grid, dims, x_ref, o_ref, state, incoming, send_sem, recv_sem):
    row, col, mine = grid.place()
    greet(grid, row, col, mine)
    started, slot = [], 0
    top, total, picked = x_ref[0], x_ref[1], x_ref[2]
    for step, dim in enumerate(dims):
        state[step, 0], state[step, 1], state[step, 2] = top, total, picked
        copies = []
        for offset in range(1, grid.sizes[dim]):
            copy = pltpu.make_async_remote_copy(
                src_ref=state.at[step],
                dst_ref=incoming.at[slot],
                send_sem=send_sem.at[slot],
                recv_sem=recv_sem.at[slot],
                device_id=grid.partner(row, col, mine, dim, grid.moved(mine, dim, offset)),
                device_id_type=MESH,
            )
            copy.start()
            copies.append((slot, copy))
            slot += 1
        for at, copy in copies:
            copy.wait_recv()
            theirs = incoming[at, 0]
            higher = jnp.maximum(top, theirs)
            total = total * jnp.exp(top - higher) + incoming[at, 1] * jnp.exp(theirs - higher)
            picked = picked + incoming[at, 2]
            top = higher
            started.append(copy)
    o_ref[0] = top + jnp.log(total)
    o_ref[1] = picked
    for copy in started:
        copy.wait_send()


def combine_stats(grid, stats, collective_id):
    dims = list(range(grid.core, -1, -1))
    slots = sum(size - 1 for size in grid.sizes)
    return pl.pallas_call(
        functools.partial(stats_kernel, grid, dims),
        out_shape=jax.ShapeDtypeStruct((2,) + stats.shape[1:], jnp.float32),
        in_specs=[pl.BlockSpec(memory_space=pltpu.VMEM)],
        out_specs=pl.BlockSpec(memory_space=pltpu.VMEM),
        scratch_shapes=[
            pltpu.VMEM((len(dims),) + stats.shape, jnp.float32),
            pltpu.VMEM((slots,) + stats.shape, jnp.float32),
            pltpu.SemaphoreType.DMA((slots,)),
            pltpu.SemaphoreType.DMA((slots,)),
        ],
        compiler_params=pltpu.CompilerParams(collective_id=collective_id, has_side_effects=True),
    )(stats)


def reduce_kernel(grid, orders, table, produce, beside, n_in, n_extra, *refs):
    ins, extra = refs[:n_in], refs[n_in : n_in + n_extra]
    refs = refs[n_in + n_extra :]
    if beside is None:
        refs = (refs[0], None) + tuple(refs[1:])
    out_ref, beside_ref, total, core_out, core_in = refs[:5]
    core_send, core_recv, send_sem, recv_sem = refs[5:9]
    outgoing, incoming = refs[9 : 9 + len(table)], refs[9 + len(table) :]
    row, col, mine = grid.place()
    greet(grid, row, col, mine)
    core, n_row = grid.core, grid.n_row
    other = 1 - mine[core]
    between = (slice(None),) * (core - 1)
    shape = total.shape[1:]
    slabs = [grid.moved(mine, 0, turn + 1) for turn in range(n_row)]
    started, waiting = [], {}

    def region(part, step, value):
        first, last, order = orders[part]
        dim, done = order[step], order[:step]
        index = []
        for d in range(core):
            index.append(value if d == dim else mine[d] if d in done else slice(None))
        return tuple(index) + (mine[core], pl.ds(first, last - first))

    def send(part, step, offset, turn=None):
        dim = orders[part][2][step]
        entry = table[part, dim, offset]
        value = grid.moved(mine, dim, offset)
        where = region(part, step, value)
        source, target, sem = outgoing[entry], incoming[entry], entry * n_row
        if turn is not None:
            where = (slabs[turn],) + where[1:]
            source, target, sem = source.at[turn], target.at[turn], sem + turn
        source[...] = total[where].astype(jnp.bfloat16)
        copy = pltpu.make_async_remote_copy(
            src_ref=source,
            dst_ref=target,
            send_sem=send_sem.at[sem],
            recv_sem=recv_sem.at[sem],
            device_id=grid.partner(row, col, mine, dim, value),
            device_id_type=MESH,
        )
        copy.start()
        started.append(copy)
        waiting[part, step, offset, turn] = copy

    def core_start(turn):
        z = slabs[turn]
        total[z] = produce(z, *ins).reshape(shape)
        core_out[turn] = total[(z,) + between + (other,)].astype(jnp.bfloat16)
        copy = pltpu.make_async_remote_copy(
            src_ref=core_out.at[turn],
            dst_ref=core_in.at[turn],
            send_sem=core_send.at[turn],
            recv_sem=core_recv.at[turn],
            device_id=grid.partner(row, col, mine, core, other),
            device_id_type=MESH,
        )
        copy.start()
        started.append(copy)
        waiting[turn] = copy

    def core_finish(turn):
        waiting[turn].wait_recv()
        where = (slabs[turn],) + between + (mine[core],)
        total[where] = total[where] + core_in[turn].astype(jnp.float32)
        for part, (_, _, order) in enumerate(orders):
            if order[0] != 0:
                for offset in range(1, grid.sizes[order[0]]):
                    send(part, 0, offset, turn)
            elif turn + 1 < n_row:
                send(part, 0, turn + 1)

    def finish(part, step):
        dim = orders[part][2][step]
        split = step == 0 and dim != 0
        for turn in range(n_row) if split else (None,):
            where = region(part, step, mine[dim])
            if split:
                where = (slabs[turn],) + where[1:]
            value = total[where]
            for offset in range(1, grid.sizes[dim]):
                waiting[part, step, offset, turn].wait_recv()
                landed = incoming[table[part, dim, offset]]
                landed = landed[turn] if split else landed[...]
                value = value + landed.astype(jnp.float32)
            total[where] = value

    for turn in range(n_row):
        core_start(turn)
        if turn:
            core_finish(turn - 1)
    core_finish(n_row - 1)
    if beside is not None:
        beside(*extra, beside_ref)
    steps = core
    turns = []
    for part in range(len(orders)):
        late = 1.5 if orders[part][2][0] == 0 else 0
        for step in range(steps):
            turns.append((step + late, part, step))
    for _, part, step in sorted(turns):
        finish(part, step)
        if step + 1 < steps:
            dim = orders[part][2][step + 1]
            for offset in range(1, grid.sizes[dim]):
                send(part, step + 1, offset)
    out_ref[...] = total[tuple(mine)]
    for copy in started:
        copy.wait_send()


def reduce_scatter(grid, produce, ins, beside, extra, beside_shape, rows, cols, plan, collective_id):
    core = grid.core
    orders = []
    for first, last, turn, row_first in plan:
        middle = grid.middle(turn)
        orders.append((first, last, [0] + middle if row_first else middle + [0]))
    table, count = semaphore_table(grid, orders)
    buffers = []
    for part, (first, last, order) in enumerate(orders):
        for step, dim in enumerate(order):
            left = tuple(grid.sizes[d] for d in range(core) if d not in order[: step + 1])
            for offset in range(1, grid.sizes[dim]):
                buffers.append(pltpu.VMEM(left + (last - first, cols), jnp.bfloat16))
    sizes = tuple(grid.sizes)
    half = pltpu.VMEM(sizes[:-1] + (rows, cols), jnp.bfloat16)
    shapes = [jax.ShapeDtypeStruct((rows, cols), jnp.float32)]
    if beside is not None:
        shapes.append(jax.ShapeDtypeStruct(beside_shape, jnp.bfloat16))
    return pl.pallas_call(
        functools.partial(
            reduce_kernel, grid, orders, table, produce, beside, len(ins), len(extra)
        ),
        out_shape=shapes,
        in_specs=[pl.BlockSpec(memory_space=pltpu.VMEM)] * (len(ins) + len(extra)),
        out_specs=[pl.BlockSpec(memory_space=pltpu.VMEM)] * len(shapes),
        scratch_shapes=[
            pltpu.VMEM(sizes + (rows, cols), jnp.float32),
            half,
            half,
            pltpu.SemaphoreType.DMA((grid.n_row,)),
            pltpu.SemaphoreType.DMA((grid.n_row,)),
            pltpu.SemaphoreType.DMA((count * grid.n_row,)),
            pltpu.SemaphoreType.DMA((count * grid.n_row,)),
        ]
        + buffers
        + buffers,
        compiler_params=pltpu.CompilerParams(
            collective_id=collective_id, has_side_effects=True, vmem_limit_bytes=LIMIT
        ),
    )(*ins, *extra)


def contract_first(left, right):
    return lax.dot_general(
        left, right, (((0,), (0,)), ((), ())), preferred_element_type=jnp.float32
    )


def query_slab(z, height, dscores_ref, pa_ref):
    return jnp.dot(
        dscores_ref[pl.ds(pl.multiple_of(z * height, height), height), :],
        pa_ref[...],
        preferred_element_type=jnp.float32,
    )


def adapter_slab(z, width, passages_ref, dpa_ref, queries_ref, dqa_ref):
    columns = pl.ds(pl.multiple_of(z * width, width), width)
    return contract_first(
        jnp.concatenate([passages_ref[:, columns], queries_ref[:, columns]], axis=0),
        jnp.concatenate([dpa_ref[...], dqa_ref[...]], axis=0),
    )


def adapt(passages_ref, adapter_ref, pa_ref):
    block = min(256, pa_ref.shape[0])

    @pl.loop(0, pa_ref.shape[0] // block)
    def _(step):
        rows = pl.ds(pl.multiple_of(step * block, block), block)
        pa_ref[rows, :] = jnp.dot(
            passages_ref[rows, :], adapter_ref[...], preferred_element_type=jnp.float32
        ).astype(jnp.bfloat16)


def passage_grad(dscores_ref, qa_ref, dpa_ref):
    block = min(256, dpa_ref.shape[0])

    @pl.loop(0, dpa_ref.shape[0] // block)
    def _(step):
        rows = pl.ds(pl.multiple_of(step * block, block), block)
        dpa_ref[rows, :] = contract_first(dscores_ref[:, rows], qa_ref[...]).astype(jnp.bfloat16)


def thirds(rows):
    unit = rows // 16
    large = (unit * 3) // 8
    if large == 0:
        half = (unit // 2) * 16
        if half == 0:
            return [(0, rows, 0, False)]
        return [(0, half, 0, False), (half, rows, 1, False)]
    return [
        (0, 16 * large, 0, False),
        (16 * large, 32 * large, 1, False),
        (32 * large, rows, 0, True),
    ]


def per_device(grid, queries, passages, adapter, positives):
    scale = adapter.shape[1] ** (-0.5)
    slab_rows = passages.shape[0]
    own_rows, width = queries.shape
    emb = adapter.shape[1]
    n = grid.n_row * grid.n_col
    n_query = own_rows * n
    here = lax.axis_index(("row", "col"))
    local_qa = jnp.dot(queries, adapter, preferred_element_type=jnp.float32).astype(jnp.bfloat16)
    cuts = [0, own_rows // 2, own_rows] if own_rows % 32 == 0 else [0, own_rows]
    qa, pa = gather(grid, local_qa, cuts, adapt, (passages, adapter), (slab_rows, emb), 0)
    scores = (
        lax.dot_general(qa, pa, (((1,), (1,)), ((), ())), preferred_element_type=jnp.float32)
        * scale
    )
    columns = here * slab_rows + jnp.arange(slab_rows, dtype=jnp.int32)
    hit = positives[:, None] == columns[None, :]
    local_max = jnp.max(scores, axis=1)
    local_pos = jnp.sum(jnp.where(hit, scores, 0.0), axis=1)
    local_sum = jnp.sum(jnp.exp(scores - local_max[:, None]), axis=1)
    stats = jnp.stack([local_max, local_sum, local_pos]).reshape(3, -1, 128)
    lse, picked = combine_stats(grid, stats, 1).reshape(2, n_query)
    probs = jnp.exp(scores - lse[:, None])
    dscores = ((probs - hit.astype(jnp.float32)) * scale).astype(jnp.bfloat16)
    dqa_own, dpa = reduce_scatter(
        grid,
        lambda z, *refs: query_slab(z, n_query // grid.n_row, *refs),
        (dscores, pa),
        lambda qa_ref, dscores_ref, dpa_ref: passage_grad(dscores_ref, qa_ref, dpa_ref),
        (qa, dscores),
        (slab_rows, emb),
        own_rows,
        emb,
        thirds(own_rows),
        2,
    )
    dqa_own = dqa_own.astype(jnp.bfloat16)
    query_grad = lax.dot_general(
        dqa_own, adapter, (((1,), (1,)), ((), ())), preferred_element_type=jnp.float32
    ).astype(jnp.bfloat16)
    (adapter_grad,) = reduce_scatter(
        grid,
        lambda z, *refs: adapter_slab(z, width // grid.n_row, *refs),
        (passages, dpa, queries, dqa_own),
        None,
        (),
        None,
        width // n,
        emb,
        thirds(width // n),
        3,
    )
    first_row = here * own_rows
    losses = lax.dynamic_slice_in_dim(lse - picked, first_row, own_rows, 0)
    return (adapter_grad, query_grad, losses)


def solution(mesh):
    grid = Grid(mesh.shape["row"], mesh.shape["col"])
    placed = (P(("row", "col"), None), P(("row", "col"), None), P(), P())
    return jax.shard_map(
        functools.partial(per_device, grid),
        mesh=mesh,
        in_specs=placed,
        out_specs=(P(("row", "col"), None), P(("row", "col"), None), P(("row", "col"))),
        check_vma=False,
    )
```

```python
import functools

import jax
import jax.numpy as jnp
from jax import lax
from jax.experimental import pallas as pl
from jax.experimental.pallas import tpu as pltpu
from jax.sharding import PartitionSpec as P

MESH = pl.DeviceIdType.MESH
LIMIT = 56 * 1024 * 1024


class Grid:
    def __init__(self, n_row, n_col):
        factors, left = [], n_col
        while left % 2 == 0:
            factors.append(2)
            left //= 2
        if left > 1:
            factors.insert(0, left)
        self.sizes = [n_row] + factors[::-1] if left == 1 else [n_row] + factors
        self.n_row, self.n_col = n_row, n_col
        self.core = len(self.sizes) - 1
        self.strides = [0] * len(self.sizes)
        stride = 1
        for dim in range(self.core, 0, -1):
            self.strides[dim] = stride
            stride *= self.sizes[dim]

    def place(self):
        row, col = lax.axis_index("row"), lax.axis_index("col")
        mine = [row]
        for dim in range(1, self.core + 1):
            mine.append(lax.rem(col // self.strides[dim], self.sizes[dim]))
        return row, col, mine

    def partner(self, row, col, mine, dim, value):
        if dim == 0:
            return (value, col)
        return (row, col + (value - mine[dim]) * self.strides[dim])

    def moved(self, mine, dim, offset):
        size = self.sizes[dim]
        return lax.rem(mine[dim] + offset + size, size)

    def middle(self, first):
        dims = list(range(1, self.core))
        first = first % max(len(dims), 1)
        return dims[first:] + dims[:first]


def greet(grid, row, col, mine):
    barrier = pltpu.get_barrier_semaphore()
    count = 0
    for dim, size in enumerate(grid.sizes):
        for offset in range(1, size):
            pl.semaphore_signal(
                barrier,
                inc=1,
                device_id=grid.partner(row, col, mine, dim, grid.moved(mine, dim, offset)),
                device_id_type=MESH,
            )
            count += 1
    pl.semaphore_wait(barrier, count)


def semaphore_table(grid, orders):
    table, count = {}, 0
    for part, (_, _, order) in enumerate(orders):
        for dim in order:
            for offset in range(1, grid.sizes[dim]):
                table[part, dim, offset] = count
                count += 1
    return table, count


def gather_kernel(grid, orders, table, beside, n_extra, x_ref, *refs):
    extra, o_ref, beside_ref = refs[:n_extra], refs[n_extra], refs[n_extra + 1]
    send_sem, recv_sem, load_sem = refs[n_extra + 2 : n_extra + 5]
    held = refs[n_extra + 5 :]
    loads = []
    for at in range(n_extra):
        load = pltpu.make_async_copy(extra[at], held[at], load_sem.at[at])
        load.start()
        loads.append(load)
    row, col, mine = grid.place()
    greet(grid, row, col, mine)
    o_ref[tuple(mine)] = x_ref[...]
    started = []

    def region(part, step, values):
        first, last, order = orders[part]
        done = order[:step]
        return o_ref.at[
            tuple(slice(None) if d in done else values[d] for d in range(len(values)))
            + (pl.ds(first, last - first),)
        ]

    def start(part, step):
        dim = orders[part][2][step]
        source = region(part, step, mine)
        for offset in range(1, grid.sizes[dim]):
            sem = table[part, dim, offset]
            copy = pltpu.make_async_remote_copy(
                src_ref=source,
                dst_ref=source,
                send_sem=send_sem.at[sem],
                recv_sem=recv_sem.at[sem],
                device_id=grid.partner(row, col, mine, dim, grid.moved(mine, dim, offset)),
                device_id_type=MESH,
            )
            copy.start()
            started.append(copy)

    def finish(part, step):
        dim = orders[part][2][step]
        for offset in range(1, grid.sizes[dim]):
            sem = table[part, dim, offset]
            theirs = list(mine)
            theirs[dim] = grid.moved(mine, dim, -offset)
            landing = region(part, step, theirs)
            pltpu.make_async_remote_copy(
                src_ref=landing,
                dst_ref=landing,
                send_sem=send_sem.at[sem],
                recv_sem=recv_sem.at[sem],
                device_id=grid.partner(row, col, mine, dim, theirs[dim]),
                device_id_type=MESH,
            ).wait_recv()

    for part in range(len(orders)):
        start(part, 0)
    for load in loads:
        load.wait()
    beside(*held, beside_ref)
    steps = len(grid.sizes)
    for step in range(steps):
        for part in range(len(orders)):
            finish(part, step)
            if step + 1 < steps:
                start(part, step + 1)
    for copy in started:
        copy.wait_send()


def gather(grid, x, cuts, beside, extra, beside_shape, collective_id):
    rows, cols = x.shape
    orders = []
    for part, (first, last) in enumerate(zip(cuts[:-1], cuts[1:])):
        orders.append((first, last, [0] + grid.middle(part) + [grid.core]))
    table, count = semaphore_table(grid, orders)
    out, made = pl.pallas_call(
        functools.partial(gather_kernel, grid, orders, table, beside, len(extra)),
        out_shape=(
            jax.ShapeDtypeStruct(tuple(grid.sizes) + (rows, cols), x.dtype),
            jax.ShapeDtypeStruct(beside_shape, jnp.bfloat16),
        ),
        in_specs=[pl.BlockSpec(memory_space=pltpu.VMEM)]
        + [pl.BlockSpec(memory_space=pl.ANY)] * len(extra),
        out_specs=[pl.BlockSpec(memory_space=pltpu.VMEM)] * 2,
        scratch_shapes=[
            pltpu.SemaphoreType.DMA((count,)),
            pltpu.SemaphoreType.DMA((count,)),
            pltpu.SemaphoreType.DMA((len(extra),)),
        ]
        + [pltpu.VMEM(array.shape, array.dtype) for array in extra],
        compiler_params=pltpu.CompilerParams(
            collective_id=collective_id, has_side_effects=True, vmem_limit_bytes=LIMIT
        ),
    )(x, *extra)
    return out.reshape(grid.n_row * grid.n_col * rows, cols), made


def stats_kernel(grid, dims, x_ref, o_ref, state, incoming, send_sem, recv_sem):
    row, col, mine = grid.place()
    greet(grid, row, col, mine)
    started, slot = [], 0
    top, total, picked = x_ref[0], x_ref[1], x_ref[2]
    for step, dim in enumerate(dims):
        state[step, 0], state[step, 1], state[step, 2] = top, total, picked
        copies = []
        for offset in range(1, grid.sizes[dim]):
            copy = pltpu.make_async_remote_copy(
                src_ref=state.at[step],
                dst_ref=incoming.at[slot],
                send_sem=send_sem.at[slot],
                recv_sem=recv_sem.at[slot],
                device_id=grid.partner(row, col, mine, dim, grid.moved(mine, dim, offset)),
                device_id_type=MESH,
            )
            copy.start()
            copies.append((slot, copy))
            slot += 1
        for at, copy in copies:
            copy.wait_recv()
            theirs = incoming[at, 0]
            higher = jnp.maximum(top, theirs)
            total = total * jnp.exp(top - higher) + incoming[at, 1] * jnp.exp(theirs - higher)
            picked = picked + incoming[at, 2]
            top = higher
            started.append(copy)
    o_ref[0] = top + jnp.log(total)
    o_ref[1] = picked
    for copy in started:
        copy.wait_send()


def combine_stats(grid, stats, collective_id):
    dims = list(range(grid.core, -1, -1))
    slots = sum(size - 1 for size in grid.sizes)
    return pl.pallas_call(
        functools.partial(stats_kernel, grid, dims),
        out_shape=jax.ShapeDtypeStruct((2,) + stats.shape[1:], jnp.float32),
        in_specs=[pl.BlockSpec(memory_space=pltpu.VMEM)],
        out_specs=pl.BlockSpec(memory_space=pltpu.VMEM),
        scratch_shapes=[
            pltpu.VMEM((len(dims),) + stats.shape, jnp.float32),
            pltpu.VMEM((slots,) + stats.shape, jnp.float32),
            pltpu.SemaphoreType.DMA((slots,)),
            pltpu.SemaphoreType.DMA((slots,)),
        ],
        compiler_params=pltpu.CompilerParams(collective_id=collective_id, has_side_effects=True),
    )(stats)


def reduce_kernel(grid, orders, table, produce, beside, n_in, n_extra, *refs):
    ins, extra = refs[:n_in], refs[n_in : n_in + n_extra]
    refs = refs[n_in + n_extra :]
    if beside is None:
        refs = (refs[0], None) + tuple(refs[1:])
    out_ref, beside_ref, total, core_out, core_in = refs[:5]
    core_send, core_recv, send_sem, recv_sem = refs[5:9]
    outgoing, incoming = refs[9 : 9 + len(table)], refs[9 + len(table) :]
    row, col, mine = grid.place()
    greet(grid, row, col, mine)
    core, n_row = grid.core, grid.n_row
    other = 1 - mine[core]
    between = (slice(None),) * (core - 1)
    shape = total.shape[1:]
    slabs = [grid.moved(mine, 0, turn + 1) for turn in range(n_row)]
    started, waiting = [], {}

    def region(part, step, value):
        first, last, order = orders[part]
        dim, done = order[step], order[:step]
        index = []
        for d in range(core):
            index.append(value if d == dim else mine[d] if d in done else slice(None))
        return tuple(index) + (mine[core], pl.ds(first, last - first))

    def send(part, step, offset, turn=None):
        dim = orders[part][2][step]
        entry = table[part, dim, offset]
        value = grid.moved(mine, dim, offset)
        where = region(part, step, value)
        source, target, sem = outgoing[entry], incoming[entry], entry * n_row
        if turn is not None:
            where = (slabs[turn],) + where[1:]
            source, target, sem = source.at[turn], target.at[turn], sem + turn
        source[...] = total[where].astype(jnp.bfloat16)
        copy = pltpu.make_async_remote_copy(
            src_ref=source,
            dst_ref=target,
            send_sem=send_sem.at[sem],
            recv_sem=recv_sem.at[sem],
            device_id=grid.partner(row, col, mine, dim, value),
            device_id_type=MESH,
        )
        copy.start()
        started.append(copy)
        waiting[part, step, offset, turn] = copy

    def core_start(turn):
        z = slabs[turn]
        total[z] = produce(z, *ins).reshape(shape)
        core_out[turn] = total[(z,) + between + (other,)].astype(jnp.bfloat16)
        copy = pltpu.make_async_remote_copy(
            src_ref=core_out.at[turn],
            dst_ref=core_in.at[turn],
            send_sem=core_send.at[turn],
            recv_sem=core_recv.at[turn],
            device_id=grid.partner(row, col, mine, core, other),
            device_id_type=MESH,
        )
        copy.start()
        started.append(copy)
        waiting[turn] = copy

    def core_finish(turn):
        waiting[turn].wait_recv()
        where = (slabs[turn],) + between + (mine[core],)
        total[where] = total[where] + core_in[turn].astype(jnp.float32)
        for part, (_, _, order) in enumerate(orders):
            if order[0] != 0:
                for offset in range(1, grid.sizes[order[0]]):
                    send(part, 0, offset, turn)
            elif turn + 1 < n_row:
                send(part, 0, turn + 1)

    def finish(part, step):
        dim = orders[part][2][step]
        split = step == 0 and dim != 0
        for turn in range(n_row) if split else (None,):
            where = region(part, step, mine[dim])
            if split:
                where = (slabs[turn],) + where[1:]
            value = total[where]
            for offset in range(1, grid.sizes[dim]):
                waiting[part, step, offset, turn].wait_recv()
                landed = incoming[table[part, dim, offset]]
                landed = landed[turn] if split else landed[...]
                value = value + landed.astype(jnp.float32)
            total[where] = value

    for turn in range(n_row):
        core_start(turn)
        if turn:
            core_finish(turn - 1)
    core_finish(n_row - 1)
    if beside is not None:
        beside(*extra, beside_ref)
    steps = core
    turns = []
    for part in range(len(orders)):
        late = 1.5 if orders[part][2][0] == 0 else 0
        for step in range(steps):
            turns.append((step + late, part, step))
    for _, part, step in sorted(turns):
        finish(part, step)
        if step + 1 < steps:
            dim = orders[part][2][step + 1]
            for offset in range(1, grid.sizes[dim]):
                send(part, step + 1, offset)
    out_ref[...] = total[tuple(mine)]
    for copy in started:
        copy.wait_send()


def reduce_scatter(grid, produce, ins, beside, extra, beside_shape, rows, cols, plan, collective_id):
    core = grid.core
    orders = []
    for first, last, turn, row_first in plan:
        middle = grid.middle(turn)
        orders.append((first, last, [0] + middle if row_first else middle + [0]))
    table, count = semaphore_table(grid, orders)
    buffers = []
    for part, (first, last, order) in enumerate(orders):
        for step, dim in enumerate(order):
            left = tuple(grid.sizes[d] for d in range(core) if d not in order[: step + 1])
            for offset in range(1, grid.sizes[dim]):
                buffers.append(pltpu.VMEM(left + (last - first, cols), jnp.bfloat16))
    sizes = tuple(grid.sizes)
    half = pltpu.VMEM(sizes[:-1] + (rows, cols), jnp.bfloat16)
    shapes = [jax.ShapeDtypeStruct((rows, cols), jnp.float32)]
    if beside is not None:
        shapes.append(jax.ShapeDtypeStruct(beside_shape, jnp.bfloat16))
    return pl.pallas_call(
        functools.partial(
            reduce_kernel, grid, orders, table, produce, beside, len(ins), len(extra)
        ),
        out_shape=shapes,
        in_specs=[pl.BlockSpec(memory_space=pltpu.VMEM)] * (len(ins) + len(extra)),
        out_specs=[pl.BlockSpec(memory_space=pltpu.VMEM)] * len(shapes),
        scratch_shapes=[
            pltpu.VMEM(sizes + (rows, cols), jnp.float32),
            half,
            half,
            pltpu.SemaphoreType.DMA((grid.n_row,)),
            pltpu.SemaphoreType.DMA((grid.n_row,)),
            pltpu.SemaphoreType.DMA((count * grid.n_row,)),
            pltpu.SemaphoreType.DMA((count * grid.n_row,)),
        ]
        + buffers
        + buffers,
        compiler_params=pltpu.CompilerParams(
            collective_id=collective_id, has_side_effects=True, vmem_limit_bytes=LIMIT
        ),
    )(*ins, *extra)


def contract_first(left, right):
    return lax.dot_general(
        left, right, (((0,), (0,)), ((), ())), preferred_element_type=jnp.float32
    )


def query_slab(z, height, dscores_ref, pa_ref):
    return jnp.dot(
        dscores_ref[pl.ds(pl.multiple_of(z * height, height), height), :],
        pa_ref[...],
        preferred_element_type=jnp.float32,
    )


def adapter_slab(z, width, passages_ref, dpa_ref, queries_ref, dqa_ref):
    columns = pl.ds(pl.multiple_of(z * width, width), width)
    return contract_first(
        jnp.concatenate([passages_ref[:, columns], queries_ref[:, columns]], axis=0),
        jnp.concatenate([dpa_ref[...], dqa_ref[...]], axis=0),
    )


def adapt(passages_ref, adapter_ref, pa_ref):
    block = min(256, pa_ref.shape[0])

    @pl.loop(0, pa_ref.shape[0] // block)
    def _(step):
        rows = pl.ds(pl.multiple_of(step * block, block), block)
        pa_ref[rows, :] = jnp.dot(
            passages_ref[rows, :], adapter_ref[...], preferred_element_type=jnp.float32
        ).astype(jnp.bfloat16)


def passage_grad(dscores_ref, qa_ref, dpa_ref):
    block = min(256, dpa_ref.shape[0])

    @pl.loop(0, dpa_ref.shape[0] // block)
    def _(step):
        rows = pl.ds(pl.multiple_of(step * block, block), block)
        dpa_ref[rows, :] = contract_first(dscores_ref[:, rows], qa_ref[...]).astype(jnp.bfloat16)


def thirds(rows):
    unit = rows // 16
    large = (unit * 3) // 8
    if large == 0:
        half = (unit // 2) * 16
        if half == 0:
            return [(0, rows, 0, False)]
        return [(0, half, 0, False), (half, rows, 1, False)]
    return [
        (0, 16 * large, 0, False),
        (16 * large, 32 * large, 1, False),
        (32 * large, rows, 0, True),
    ]


def per_device(grid, queries, passages, adapter, positives):
    scale = adapter.shape[1] ** (-0.5)
    slab_rows = passages.shape[0]
    own_rows, width = queries.shape
    emb = adapter.shape[1]
    n = grid.n_row * grid.n_col
    n_query = own_rows * n
    here = lax.axis_index(("row", "col"))
    local_qa = jnp.dot(queries, adapter, preferred_element_type=jnp.float32).astype(jnp.bfloat16)
    cuts = [0, own_rows // 2, own_rows] if own_rows % 32 == 0 else [0, own_rows]
    qa, pa = gather(grid, local_qa, cuts, adapt, (passages, adapter), (slab_rows, emb), 0)
    scores = (
        lax.dot_general(qa, pa, (((1,), (1,)), ((), ())), preferred_element_type=jnp.float32)
        * scale
    )
    columns = here * slab_rows + jnp.arange(slab_rows, dtype=jnp.int32)
    hit = positives[:, None] == columns[None, :]
    local_max = jnp.max(scores, axis=1)
    local_pos = jnp.sum(jnp.where(hit, scores, 0.0), axis=1)
    local_sum = jnp.sum(jnp.exp(scores - local_max[:, None]), axis=1)
    stats = jnp.stack([local_max, local_sum, local_pos]).reshape(3, -1, 128)
    lse, picked = combine_stats(grid, stats, 1).reshape(2, n_query)
    probs = jnp.exp(scores - lse[:, None])
    dscores = ((probs - hit.astype(jnp.float32)) * scale).astype(jnp.bfloat16)
    dqa_own, dpa = reduce_scatter(
        grid,
        lambda z, *refs: query_slab(z, n_query // grid.n_row, *refs),
        (dscores, pa),
        lambda qa_ref, dscores_ref, dpa_ref: passage_grad(dscores_ref, qa_ref, dpa_ref),
        (qa, dscores),
        (slab_rows, emb),
        own_rows,
        emb,
        thirds(own_rows),
        2,
    )
    dqa_own = dqa_own.astype(jnp.bfloat16)
    query_grad = lax.dot_general(
        dqa_own, adapter, (((1,), (1,)), ((), ())), preferred_element_type=jnp.float32
    ).astype(jnp.bfloat16)
    (adapter_grad,) = reduce_scatter(
        grid,
        lambda z, *refs: adapter_slab(z, width // grid.n_row, *refs),
        (passages, dpa, queries, dqa_own),
        None,
        (),
        None,
        width // n,
        emb,
        thirds(width // n),
        3,
    )
    first_row = here * own_rows
    losses = lax.dynamic_slice_in_dim(lse - picked, first_row, own_rows, 0)
    return (adapter_grad, query_grad, losses)


def solution(mesh):
    grid = Grid(mesh.shape["row"], mesh.shape["col"])
    placed = (P(("row", "col"), None), P(("row", "col"), None), P(), P())
    return jax.shard_map(
        functools.partial(per_device, grid),
        mesh=mesh,
        in_specs=placed,
        out_specs=(P(("row", "col"), None), P(("row", "col"), None), P(("row", "col"))),
        check_vma=False,
    )
```
